32 devices in a mesh: tm: 8 (over z, y), freq: 4 (over x, core).
Axes of the slice: x: 2, y: 2, z: 4, core: 2. Of those that a mesh axis runs over, the one named last changes fastest.
Arguments:
- visibility: float32 [64, 2, 4096, 1024], P('freq', None, 'tm'), may hold values from -6 to 6
- codebook: bfloat16 [16, 8, 64, 128], replicated, may hold values from -0.1875 to 0.1875
- block_index: int32 [8, 64, 16, 16], P('tm', 'freq'), may hold values from -1 to 7, as said below
- block_scale: float32 [8, 64, 16, 16], P('tm', 'freq'), may hold values from 0.5 to 2
- fg_basis: float32 [16, 64, 64], replicated, may hold values from -0.75 to 0.75
- fg_count: int32 [8], P('tm'), may hold values from 1 to 32
Outputs:
- filtered: float32 [8, 64, 16, 128], P('tm', 'freq')
The draws below stay inside these ranges and needn't reach their ends.
Inputs may be any that keep to these rules, and one draw needn't show every extreme that they name: `block_index`: -1 marks an absent block; block (k, f, j, l) is absent whenever 64 * l + 63 < 127 * k; other entries name a pattern.
All inputs are finite; a program needn't handle non-finite values.
Results may differ from the reference program's by a relative error of at most 0.014.
Values may be sent and summed in bfloat16 or wider, within the bound.
A program may use at most 128 MiB of HBM per device.

```python
import math
import jax
import jax.numpy as jnp
from jax import lax

TIME_SAMPLES = 4096
BASELINE_COUNT = 1024
CHANNEL_COUNT = 64
BLOCK_WIDTH = 64
PATTERN_CODES = 8
MODES = 8
MSTEP = 127
MULTIPOLE_BLOCKS = 16
BBLOCKS = 16


def draw_block_index(key, part):
    code_draw = jax.random.randint(key, (MODES, CHANNEL_COUNT, BBLOCKS, MULTIPOLE_BLOCKS), 0, PATTERN_CODES, dtype=jnp.int32)
    mode_value = MSTEP * jnp.arange(MODES, dtype=jnp.int32)
    lblock_ids = jnp.arange(MULTIPOLE_BLOCKS, dtype=jnp.int32)
    bblock_ids = jnp.arange(BBLOCKS, dtype=jnp.int32)
    above_mode = lblock_ids[None, :] * BLOCK_WIDTH + BLOCK_WIDTH - 1 >= mode_value[:, None]
    in_reach = lblock_ids[None, :] <= MULTIPOLE_BLOCKS // 4 + bblock_ids[:, None]
    present = above_mode[:, None, None, :] & in_reach[None, None, :, :]
    return jnp.where(present, code_draw, -1).astype(jnp.int32)


def touch_ends(values, stream_key, low, top_value):
    longest = values.shape.index(max(values.shape))
    spots = []
    for shift in (0, 1):
        where = [jax.random.randint(jax.random.fold_in(stream_key, axis), (), 0, length) for axis, length in enumerate(values.shape)]
        where[longest] = (where[longest] + shift) % values.shape[longest]
        spots.append(tuple(where))
    return values.at[spots[0]].set(low).at[spots[1]].set(top_value)


def levels(stream_key, shape, pieces, low, high):
    loudness = 1.0
    for axis_at, shards_of in pieces:
        steps = jax.random.uniform(jax.random.fold_in(jax.random.fold_in(stream_key, 6), axis_at), (shards_of,), jnp.float32, low / len(pieces), high / len(pieces))
        loudness = loudness * jnp.repeat(jnp.exp(steps), shape[axis_at] // shards_of).reshape((-1,) + (1,) * (len(shape) - 1 - axis_at))
    return loudness


def bell_draw(key, dims, scale, limit, cuts=(), kind=jnp.bfloat16):
    level = levels(key, dims, cuts, -0.22, 0.18) if cuts else 1.0
    array = jax.random.normal(key, dims, jnp.float32) * scale * level
    return jnp.minimum(jnp.maximum(array, -limit), limit).astype(kind)


def setup_inputs(seed: int = 0) -> dict:
    keys = jax.random.split(jax.random.key(seed), 7)
    visibility = bell_draw(keys[0], (CHANNEL_COUNT, 2, TIME_SAMPLES, BASELINE_COUNT), 1.0, 6.0, ((0, 4), (2, 8)), jnp.float32)
    codebook = bell_draw(keys[1], (MULTIPOLE_BLOCKS, PATTERN_CODES, BLOCK_WIDTH, 2 * BLOCK_WIDTH), BASELINE_COUNT ** -0.5, 0.1875)
    block_index = draw_block_index(jax.random.fold_in(keys[6], 71), 0)
    block_scale = jnp.clip(jnp.exp(math.log(2.0) - 1.3862944 * jax.random.uniform(keys[3], (MODES, CHANNEL_COUNT, BBLOCKS, MULTIPOLE_BLOCKS), jnp.float32) ** levels(keys[3], (MODES, CHANNEL_COUNT, BBLOCKS, MULTIPOLE_BLOCKS), ((0, 8), (1, 4)), -0.2, 0.2)), 0.5, 2.0)
    fg_basis = bell_draw(keys[4], (MULTIPOLE_BLOCKS, CHANNEL_COUNT, CHANNEL_COUNT), CHANNEL_COUNT ** -0.5, 0.75, (), jnp.float32)
    fg_count = touch_ends(jax.random.randint(keys[5], (MODES,), 1, CHANNEL_COUNT // 2 + 1), jax.random.fold_in(keys[5], 1), 1, (CHANNEL_COUNT // 2 + 1) - 1).astype(jnp.int32)
    return {"visibility": visibility, "codebook": codebook, "block_index": block_index, "block_scale": block_scale, "fg_basis": fg_basis, "fg_count": fg_count}


def realify(codebook):
    half = codebook.shape[-1] // 2
    real_part = codebook[..., :half]
    imag_part = codebook[..., half:]
    upper = jnp.concatenate([real_part, -imag_part], axis=-1)
    lower = jnp.concatenate([imag_part, real_part], axis=-1)
    return jnp.concatenate([upper, lower], axis=-2)


def reference(visibility, codebook, block_index, block_scale, fg_basis, fg_count):
    selected = (MSTEP * jnp.arange(MODES, dtype=jnp.int32)).astype(jnp.int32)
    norm_factor = float(TIME_SAMPLES) ** -0.5

    def transform(channel):
        spectrum_re = jnp.fft.rfft(channel[0], axis=0)[selected]
        spectrum_im = jnp.fft.rfft(channel[1], axis=0)[selected]
        real_part = jnp.real(spectrum_re) - jnp.imag(spectrum_im)
        imag_part = jnp.imag(spectrum_re) + jnp.real(spectrum_im)
        return jnp.stack([real_part, imag_part], axis=1) * norm_factor

    spectra = lax.map(transform, visibility)
    spectra = jnp.transpose(spectra, (1, 0, 2, 3)).astype(jnp.bfloat16)
    code_matrix = realify(codebook).astype(jnp.float32)
    pattern_ids = jnp.arange(PATTERN_CODES, dtype=jnp.int32)
    mode_ids = jnp.arange(CHANNEL_COUNT, dtype=jnp.int32)

    def project(items):
        spectrum, index_rows, scale_rows, count = items
        vectors = spectrum.reshape(CHANNEL_COUNT, 2, BBLOCKS, BLOCK_WIDTH)
        vectors = jnp.transpose(vectors, (0, 2, 1, 3)).reshape(CHANNEL_COUNT, BBLOCKS, 2 * BLOCK_WIDTH).astype(jnp.float32)
        block_selector = jnp.where(index_rows[..., None] == pattern_ids, scale_rows[..., None], jnp.float32(0.0))
        combined = jnp.einsum("fblp,fbi->flpi", block_selector, vectors, precision=lax.Precision.HIGHEST)
        projected = jnp.einsum("flpi,lpij->flj", combined, code_matrix, precision=lax.Precision.HIGHEST)
        projected = lax.optimization_barrier(projected.astype(jnp.bfloat16)).astype(jnp.float32)
        filtered = jnp.einsum("lfk,flj->klj", fg_basis, projected, precision=lax.Precision.HIGHEST)
        retained = mode_ids >= count
        return jnp.where(retained[:, None, None], filtered, jnp.float32(0.0))

    return lax.map(project, (spectra, block_index, block_scale, fg_count))
```

```python
import functools
import math

import jax
import jax.numpy as jnp
import numpy as np
from jax import lax
from jax.experimental import pallas as pl
from jax.experimental.pallas import tpu as pltpu
from jax.sharding import PartitionSpec as P

ELLS = 1024
LANES = 256
SUB = 8
MESH = pl.DeviceIdType.MESH
NT = (((1,), (1,)), ((), ()))


def phase_tables(parts, time_dev, modes_all):
    period = parts * time_dev
    step = 2 * (ELLS // (2 * modes_all)) - 1
    modes = step * np.arange(modes_all, dtype=np.int64)
    times = np.arange(period, dtype=np.int64)
    angle = (modes[:, None] * times[None, :] % period) * (2.0 * math.pi / period)
    cosine = np.cos(angle).reshape(modes_all, parts, time_dev).transpose(1, 0, 2)
    sine = np.sin(angle).reshape(modes_all, parts, time_dev).transpose(1, 0, 2)
    real_rows = np.concatenate([cosine, sine], axis=2)
    imag_rows = np.concatenate([-sine, cosine], axis=2)
    return np.concatenate([real_rows, imag_rows], axis=1).astype(jnp.bfloat16)


def kernel(
    n_tm, n_fr, norm,
    tab_hbm, vis, cb_hbm, idx_hbm, scl_hbm, bas_hbm, count,
    out,
    tab, cb, idx, scl, bas, vbuf, acc, send, recv, idx_t, scl_t, sel, vec, comb, filt, gath,
    small_sem, vis_sem, send_sem, recv_sem, gsend_sem, grecv_sem,
):
    tm = lax.axis_index("tm")
    fr = lax.axis_index("freq")
    modes = tab.shape[0] // 2
    samples = vbuf.shape[2]
    chans = vis.shape[0]
    halves = chans // SUB
    lane_groups = vis.shape[3] // LANES
    groups = lane_groups * halves
    blocks = vec.shape[1]
    bands, codes = cb.shape[0], cb.shape[1]
    f32, bf16 = jnp.float32, jnp.bfloat16

    smalls = [
        pltpu.make_async_copy(src, dst, small_sem.at[i])
        for i, (src, dst) in enumerate(
            ((idx_hbm, idx), (scl_hbm, scl), (tab_hbm.at[tm], tab), (bas_hbm, bas), (cb_hbm, cb))
        )
    ]

    def fetch(g, slot):
        lanes = pl.ds(pl.multiple_of((g // halves) * LANES, LANES), LANES)
        chan = (g % halves) * SUB + slot
        return pltpu.make_async_copy(
            vis.at[chan, :, :, lanes], vbuf.at[slot], vis_sem.at[slot]
        )

    for copy in smalls[:3]:
        copy.start()
    for slot in range(SUB):
        fetch(0, slot).start()
    for copy in smalls[3:]:
        copy.start()

    barrier = pltpu.get_barrier_semaphore()

    @pl.loop(1, n_tm)
    def _(d):
        peer = lax.rem(tm + d, n_tm)
        pl.semaphore_signal(barrier, inc=1, device_id={"tm": peer}, device_id_type=MESH)

    for d in range(1, n_fr):
        peer = lax.rem(fr + d, n_fr)
        pl.semaphore_signal(barrier, inc=1, device_id={"freq": peer}, device_id_type=MESH)

    smalls[0].wait()
    smalls[1].wait()
    wide = blocks * chans
    eye = (
        lax.broadcasted_iota(jnp.int32, (bands, bands), 0)
        == lax.broadcasted_iota(jnp.int32, (bands, bands), 1)
    ).astype(f32).astype(bf16)
    for src, dst in ((idx, idx_t), (scl, scl_t)):
        rows = jnp.concatenate([src[:, j, :] for j in range(blocks)], axis=0)
        rows = rows.astype(f32).astype(bf16)
        dst[...] = lax.dot_general(eye, rows, NT, preferred_element_type=f32)
    same_chan = (
        lax.broadcasted_iota(jnp.int32, (chans, wide), 1) % chans
        == lax.broadcasted_iota(jnp.int32, (chans, wide), 0)
    )

    @pl.loop(0, bands)
    def _(l):
        which = jnp.broadcast_to(idx_t[pl.ds(l, 1), :], (chans, wide))
        which = jnp.where(same_chan, which, f32(-1.0))
        scale = jnp.broadcast_to(scl_t[pl.ds(l, 1), :], (chans, wide))
        for p in range(codes):
            row, col = (p // 2) * chans, (p % 2) * wide
            sel[l, row : row + chans, col : col + wide] = jnp.where(
                which == f32(p), scale, f32(0.0)
            ).astype(bf16)

    smalls[2].wait()
    pl.semaphore_wait(barrier, n_tm - 1 + n_fr - 1)

    def take(lane_group):
        parts = []
        for half in range(halves):
            g = lane_group * halves + half
            pltpu.make_async_copy(recv.at[g], recv.at[g], recv_sem.at[g]).wait()
            parts.append(jnp.sum(recv[g].astype(f32), axis=0))
        real = jnp.concatenate([part[:SUB] for part in parts], axis=0)
        imag = jnp.concatenate([part[SUB:] for part in parts], axis=0)
        left = lax.broadcasted_iota(jnp.int32, (chans, 128), 1) < 64
        zero = jnp.zeros((chans, 128), f32)
        for pair in range(LANES // 128):
            r = real[:, pair * 128 : pair * 128 + 128]
            i = imag[:, pair * 128 : pair * 128 + 128]
            rr, ri = pltpu.roll(r, 64, 1), pltpu.roll(i, 64, 1)
            even = lane_group * (LANES // 64) + 2 * pair

            def put(first, j, a, b):
                if first:
                    a, b = jnp.where(left, a, zero), jnp.where(left, b, zero)
                else:
                    a, b = jnp.where(left, zero, a), jnp.where(left, zero, b)
                vec[0 if first else 1, j] = jnp.concatenate([a, b], axis=1).astype(bf16)

            put(True, even, r, i)
            put(False, even, rr, ri)
            put(True, even + 1, rr, ri)
            put(False, even + 1, r, i)

    @pl.loop(0, lane_groups)
    def _(lane_group):
        @pl.loop(0, halves)
        def _(half):
            g = lane_group * halves + half
            for slot in range(SUB):
                fetch(g, slot).wait()
                block = vbuf[slot].reshape(2 * samples, LANES).astype(bf16)
                sums = jnp.dot(tab[...], block, preferred_element_type=f32)
                acc[:, slot, :] = sums[:modes]
                acc[:, SUB + slot, :] = sums[modes:]

                @pl.when(g + 1 < groups)
                def _():
                    fetch(g + 1, slot).start()

            send[g] = (acc[...] * f32(norm)).astype(bf16)
            pltpu.make_async_copy(send.at[g, tm], recv.at[g, tm], recv_sem.at[g]).start()

            @pl.loop(1, n_tm)
            def _(d):
                peer = lax.rem(tm + d, n_tm)
                pltpu.make_async_remote_copy(
                    src_ref=send.at[g, peer],
                    dst_ref=recv.at[g, tm],
                    send_sem=send_sem.at[g],
                    recv_sem=recv_sem.at[g],
                    device_id={"tm": peer},
                    device_id_type=MESH,
                ).start()

        @pl.when(lane_group > 0)
        def _():
            take(lane_group - 1)

    smalls[3].wait()
    smalls[4].wait()
    part = bands // 2
    all_chans = bas.shape[1]
    rows = chans * part
    pick = (
        lax.broadcasted_iota(jnp.int32, (rows, all_chans), 1)
        == lax.broadcasted_iota(jnp.int32, (rows, all_chans), 0) // part + fr * chans
    ).astype(f32).astype(bf16)
    basis = bas[...].reshape(bands * all_chans, all_chans).astype(bf16)
    spread = lax.dot_general(pick, basis, NT, preferred_element_type=f32)
    same_band = (
        lax.broadcasted_iota(jnp.int32, spread.shape, 1) // all_chans % part
        == lax.broadcasted_iota(jnp.int32, spread.shape, 0) % part
    )
    filt[...] = jnp.where(same_band, spread, f32(0.0)).astype(bf16)

    take(lane_groups - 1)

    vectors = vec[...].reshape(2 * wide, LANES)
    left = lax.broadcasted_iota(jnp.int32, (chans, 128), 1) < 64
    pairs = codes // 2

    def share(h, d):
        peer = lax.rem(fr + d, n_fr)
        mine = gath.at[fr, pl.ds(h * part, part)]
        return pltpu.make_async_remote_copy(
            src_ref=mine,
            dst_ref=mine,
            send_sem=gsend_sem.at[h, d - 1],
            recv_sem=grecv_sem.at[h, d - 1],
            device_id={"freq": peer},
            device_id_type=MESH,
        )

    for h in range(2):
        chosen = sel[h * part : (h + 1) * part].reshape(part * pairs * chans, 2 * wide)
        comb[...] = (
            jnp.dot(chosen, vectors, preferred_element_type=f32)
            .astype(bf16)
            .reshape(part, pairs * chans, LANES)
        )
        for k in range(part):
            c = comb[k]
            lhs = jnp.concatenate(
                [
                    jnp.concatenate(
                        [c[p * chans : (p + 1) * chans, o : o + 128] for p in range(pairs)], axis=1
                    )
                    for o in (0, 128)
                ],
                axis=0,
            )
            weights = cb[h * part + k].reshape(codes * 64, 128)
            both = jnp.dot(lhs, weights, preferred_element_type=f32)
            upper, lower = both[:chans], both[chans:]
            projected = jnp.where(left, upper, -upper) + pltpu.roll(lower, 64, 1)
            gath[fr, h * part + k] = projected.astype(bf16)
        for d in range(1, n_fr):
            share(h, d).start()

    kept = (
        lax.broadcasted_iota(jnp.int32, (chans, part, 128), 0) + fr * chans >= count[0]
    )
    for h in range(2):
        for d in range(1, n_fr):
            share(h, d).wait_recv()
        rows_in = jnp.concatenate(
            [gath[s, h * part + k] for k in range(part) for s in range(n_fr)], axis=0
        )
        depth = part * all_chans
        got = jnp.dot(
            filt[:, h * depth : (h + 1) * depth], rows_in, preferred_element_type=f32
        ).reshape(chans, part, 128)
        out[:, h * part : (h + 1) * part, :] = jnp.where(kept, got, f32(0.0))

    for h in range(2):
        for d in range(1, n_fr):
            share(h, d).wait_send()

    @pl.loop(0, groups)
    def _(g):
        sent = send.at[g, pl.ds(0, n_tm - 1)]
        pltpu.make_async_copy(sent, sent, send_sem.at[g]).wait()


def local(n_tm, n_fr, visibility, codebook, block_index, block_scale, fg_basis, fg_count):
    chans, _, time_dev, base_all = visibility.shape
    modes_all = block_index.shape[0] * n_tm
    bands, codes, block_len, width = codebook.shape
    blocks = base_all // block_len
    all_chans = fg_basis.shape[1]
    groups = base_all // LANES * (chans // SUB)
    wide = blocks * chans
    norm = float(time_dev * n_tm) ** -0.5
    tables = jnp.asarray(phase_tables(n_tm, time_dev, modes_all))
    anywhere = pl.BlockSpec(memory_space=pl.ANY)
    f32, bf16 = jnp.float32, jnp.bfloat16
    out = pl.pallas_call(
        functools.partial(kernel, n_tm, n_fr, norm),
        out_shape=jax.ShapeDtypeStruct((chans, bands, width), f32),
        in_specs=[anywhere] * 6 + [pl.BlockSpec(memory_space=pltpu.SMEM)],
        out_specs=pl.BlockSpec(memory_space=pltpu.VMEM),
        scratch_shapes=[
            pltpu.VMEM(tables.shape[1:], bf16),
            pltpu.VMEM(codebook.shape, bf16),
            pltpu.VMEM(block_index.shape[1:], jnp.int32),
            pltpu.VMEM(block_scale.shape[1:], f32),
            pltpu.VMEM(fg_basis.shape, f32),
            pltpu.VMEM((SUB, 2, time_dev, LANES), f32),
            pltpu.VMEM((modes_all, 2 * SUB, LANES), f32),
            pltpu.VMEM((groups, n_tm, 2 * SUB, LANES), bf16),
            pltpu.VMEM((groups, n_tm, 2 * SUB, LANES), bf16),
            pltpu.VMEM((bands, wide), f32),
            pltpu.VMEM((bands, wide), f32),
            pltpu.VMEM((bands, codes // 2 * chans, 2 * wide), bf16),
            pltpu.VMEM((2, blocks, chans, LANES), bf16),
            pltpu.VMEM((bands // 2, codes // 2 * chans, LANES), bf16),
            pltpu.VMEM((chans * (bands // 2), bands * all_chans), bf16),
            pltpu.VMEM((n_fr, bands, chans, width), bf16),
            pltpu.SemaphoreType.DMA((5,)),
            pltpu.SemaphoreType.DMA((SUB,)),
            pltpu.SemaphoreType.DMA((groups,)),
            pltpu.SemaphoreType.DMA((groups,)),
            pltpu.SemaphoreType.DMA((2, n_fr - 1)),
            pltpu.SemaphoreType.DMA((2, n_fr - 1)),
        ],
        compiler_params=pltpu.CompilerParams(
            collective_id=0, has_side_effects=True, vmem_limit_bytes=48 * 1024 * 1024
        ),
        name="mmode",
    )(
        tables,
        visibility,
        codebook,
        block_index.reshape(block_index.shape[1:]),
        block_scale.reshape(block_scale.shape[1:]),
        fg_basis,
        fg_count,
    )
    return out[None]


def solution(mesh):
    placed = (
        P("freq", None, "tm", None),
        P(),
        P("tm", "freq", None, None),
        P("tm", "freq", None, None),
        P(),
        P("tm"),
    )
    return jax.shard_map(
        functools.partial(local, mesh.shape["tm"], mesh.shape["freq"]),
        mesh=mesh,
        in_specs=placed,
        out_specs=P("tm", "freq", None, None),
        check_vma=False,
    )
```

```python
import functools
import math

import jax
import jax.numpy as jnp
import numpy as np
from jax import lax
from jax.experimental import pallas as pl
from jax.experimental.pallas import tpu as pltpu
from jax.sharding import PartitionSpec as P

ELLS = 1024
LANES = 256
SUB = 8
BATCH = 4
DEPTH = 4
MESH = pl.DeviceIdType.MESH
NT = (((1,), (1,)), ((), ()))


def phase_tables(parts, time_dev, modes_all):
    period = parts * time_dev
    step = 2 * (ELLS // (2 * modes_all)) - 1
    modes = step * np.arange(modes_all, dtype=np.int64)
    times = np.arange(period, dtype=np.int64)
    angle = (modes[:, None] * times[None, :] % period) * (2.0 * math.pi / period)
    cosine = np.cos(angle).reshape(modes_all, parts, time_dev).transpose(1, 0, 2)
    sine = np.sin(angle).reshape(modes_all, parts, time_dev).transpose(1, 0, 2)
    real_rows = np.concatenate([cosine, sine], axis=2)
    imag_rows = np.concatenate([-sine, cosine], axis=2)
    return np.concatenate([real_rows, imag_rows], axis=1).astype(np.float32)


def kernel(
    n_tm, n_fr, norm,
    tab_hbm, vis, cb_hbm, idx_hbm, scl_hbm, bas_hbm, cnt_hbm,
    out,
    tab, cb, idx, scl, bas, tab_in, count, vbuf, acc, send, recv, idx_t, scl_t, sel, vec, comb, filt, gath,
    small_sem, vis_sem, send_sem, recv_sem, gsend_sem, grecv_sem,
):
    tm = lax.axis_index("tm")
    fr = lax.axis_index("freq")
    modes = tab.shape[0] // 2
    samples = vbuf.shape[3]
    chans = vis.shape[0]
    halves = chans // SUB
    lane_groups = vis.shape[3] // LANES
    groups = lane_groups * halves
    piece = min(256, samples)
    blocks = vec.shape[1]
    bands, codes = cb.shape[0], cb.shape[1]
    f32, bf16 = jnp.float32, jnp.bfloat16

    smalls = [
        pltpu.make_async_copy(src, dst, small_sem.at[i])
        for i, (src, dst) in enumerate(
            (
                (idx_hbm, idx), (scl_hbm, scl), (tab_hbm.at[tm], tab_in), (bas_hbm, bas), (cb_hbm, cb),
                (cnt_hbm, count),
            )
        )
    ]

    def fetch(step, slot):
        per_group = SUB // BATCH
        g = step // per_group
        lanes = pl.ds(pl.multiple_of((g // halves) * LANES, LANES), LANES)
        chan = (g % halves) * SUB + (step % per_group) * BATCH
        return pltpu.make_async_copy(
            vis.at[pl.ds(chan, BATCH), :, :, lanes], vbuf.at[slot], vis_sem.at[slot]
        )

    for copy in smalls[:3]:
        copy.start()
    for slot in range(DEPTH):
        fetch(slot, slot).start()
    for copy in smalls[3:]:
        copy.start()

    barrier = pltpu.get_barrier_semaphore()

    @pl.loop(1, n_tm)
    def _(d):
        peer = lax.rem(tm + d, n_tm)
        pl.semaphore_signal(barrier, inc=1, device_id={"tm": peer}, device_id_type=MESH)

    for d in range(1, n_fr):
        peer = lax.rem(fr + d, n_fr)
        pl.semaphore_signal(barrier, inc=1, device_id={"freq": peer}, device_id_type=MESH)

    smalls[0].wait()
    smalls[1].wait()
    wide = blocks * chans
    eye = (
        lax.broadcasted_iota(jnp.int32, (bands, bands), 0)
        == lax.broadcasted_iota(jnp.int32, (bands, bands), 1)
    ).astype(f32).astype(bf16)
    for src, dst in ((idx, idx_t), (scl, scl_t)):
        rows = jnp.concatenate([src[:, j, :] for j in range(blocks)], axis=0)
        rows = rows.astype(f32).astype(bf16)
        dst[...] = lax.dot_general(eye, rows, NT, preferred_element_type=f32)
    same_chan = (
        lax.broadcasted_iota(jnp.int32, (chans, wide), 1) % chans
        == lax.broadcasted_iota(jnp.int32, (chans, wide), 0)
    )

    @pl.loop(0, bands)
    def _(l):
        which = jnp.broadcast_to(idx_t[pl.ds(l, 1), :], (chans, wide))
        which = jnp.where(same_chan, which, f32(-1.0))
        scale = jnp.broadcast_to(scl_t[pl.ds(l, 1), :], (chans, wide))
        for p in range(codes):
            row, col = (p // 2) * chans, (p % 2) * wide
            sel[l, row : row + chans, col : col + wide] = jnp.where(
                which == f32(p), scale, f32(0.0)
            ).astype(bf16)

    smalls[2].wait()
    tab[...] = tab_in[...].astype(bf16)
    pl.semaphore_wait(barrier, n_tm - 1 + n_fr - 1)

    def take(lane_group):
        parts = []
        for half in range(halves):
            g = lane_group * halves + half
            pltpu.make_async_copy(recv.at[g], recv.at[g], recv_sem.at[g]).wait()
            parts.append(jnp.sum(recv[g].astype(f32), axis=0))
        real = jnp.concatenate([part[:SUB] for part in parts], axis=0)
        imag = jnp.concatenate([part[SUB:] for part in parts], axis=0)
        left = lax.broadcasted_iota(jnp.int32, (chans, 128), 1) < 64
        zero = jnp.zeros((chans, 128), f32)
        for pair in range(LANES // 128):
            r = real[:, pair * 128 : pair * 128 + 128]
            i = imag[:, pair * 128 : pair * 128 + 128]
            rr, ri = pltpu.roll(r, 64, 1), pltpu.roll(i, 64, 1)
            even = lane_group * (LANES // 64) + 2 * pair

            def put(first, j, a, b):
                if first:
                    a, b = jnp.where(left, a, zero), jnp.where(left, b, zero)
                else:
                    a, b = jnp.where(left, zero, a), jnp.where(left, zero, b)
                vec[0 if first else 1, j] = jnp.concatenate([a, b], axis=1).astype(bf16)

            put(True, even, r, i)
            put(False, even, rr, ri)
            put(True, even + 1, rr, ri)
            put(False, even + 1, r, i)

    @pl.loop(0, lane_groups)
    def _(lane_group):
        @pl.loop(0, halves)
        def _(half):
            g = lane_group * halves + half
            for part in range(SUB // BATCH):
                step = g * (SUB // BATCH) + part
                slot = lax.rem(step, DEPTH)
                fetch(step, slot).wait()
                for i in range(BATCH):
                    sums = jnp.zeros((2 * modes, LANES), f32)
                    for c in range(2):
                        for t in range(0, samples, piece):
                            block = vbuf[slot, i, c, t : t + piece, :].astype(bf16)
                            table = tab[:, c * samples + t : c * samples + t + piece]
                            sums += jnp.dot(table, block, preferred_element_type=f32)
                    chan = part * BATCH + i
                    acc[:, chan, :] = sums[:modes]
                    acc[:, SUB + chan, :] = sums[modes:]

                @pl.when(step + DEPTH < groups * (SUB // BATCH))
                def _():
                    fetch(step + DEPTH, slot).start()

            send[g] = (acc[...] * f32(norm)).astype(bf16)
            pltpu.make_async_copy(send.at[g, tm], recv.at[g, tm], recv_sem.at[g]).start()

            @pl.loop(1, n_tm)
            def _(d):
                peer = lax.rem(tm + d, n_tm)
                pltpu.make_async_remote_copy(
                    src_ref=send.at[g, peer],
                    dst_ref=recv.at[g, tm],
                    send_sem=send_sem.at[g],
                    recv_sem=recv_sem.at[g],
                    device_id={"tm": peer},
                    device_id_type=MESH,
                ).start()

        @pl.when(lane_group > 0)
        def _():
            take(lane_group - 1)

    smalls[3].wait()
    smalls[4].wait()
    smalls[5].wait()
    part = bands // 2
    all_chans = bas.shape[1]
    rows = chans * part
    pick = (
        lax.broadcasted_iota(jnp.int32, (rows, all_chans), 1)
        == lax.broadcasted_iota(jnp.int32, (rows, all_chans), 0) // part + fr * chans
    ).astype(f32).astype(bf16)
    basis = bas[...].reshape(bands * all_chans, all_chans).astype(bf16)
    spread = lax.dot_general(pick, basis, NT, preferred_element_type=f32)
    same_band = (
        lax.broadcasted_iota(jnp.int32, spread.shape, 1) // all_chans % part
        == lax.broadcasted_iota(jnp.int32, spread.shape, 0) % part
    )
    filt[...] = jnp.where(same_band, spread, f32(0.0)).astype(bf16)

    take(lane_groups - 1)

    vectors = vec[...].reshape(2 * wide, LANES)
    left = lax.broadcasted_iota(jnp.int32, (chans, 128), 1) < 64
    pairs = codes // 2

    def share(h, d):
        peer = lax.rem(fr + d, n_fr)
        mine = gath.at[fr, pl.ds(h * part, part)]
        return pltpu.make_async_remote_copy(
            src_ref=mine,
            dst_ref=mine,
            send_sem=gsend_sem.at[h, d - 1],
            recv_sem=grecv_sem.at[h, d - 1],
            device_id={"freq": peer},
            device_id_type=MESH,
        )

    for h in range(2):
        chosen = sel[h * part : (h + 1) * part].reshape(part * pairs * chans, 2 * wide)
        comb[...] = (
            jnp.dot(chosen, vectors, preferred_element_type=f32)
            .astype(bf16)
            .reshape(part, pairs * chans, LANES)
        )
        for k in range(part):
            c = comb[k]
            lhs = jnp.concatenate(
                [
                    jnp.concatenate(
                        [c[p * chans : (p + 1) * chans, o : o + 128] for p in range(pairs)], axis=1
                    )
                    for o in (0, 128)
                ],
                axis=0,
            )
            weights = cb[h * part + k].reshape(codes * 64, 128)
            both = jnp.dot(lhs, weights, preferred_element_type=f32)
            upper, lower = both[:chans], both[chans:]
            projected = jnp.where(left, upper, -upper) + pltpu.roll(lower, 64, 1)
            gath[fr, h * part + k] = projected.astype(bf16)
        for d in range(1, n_fr):
            share(h, d).start()

    mode_index = lax.broadcasted_iota(jnp.int32, (chans, part, 128), 0) + fr * chans
    kept = mode_index >= count[...].reshape(1, 1, 1)
    for h in range(2):
        for d in range(1, n_fr):
            share(h, d).wait_recv()
        rows_in = jnp.concatenate(
            [gath[s, h * part + k] for k in range(part) for s in range(n_fr)], axis=0
        )
        depth = part * all_chans
        got = jnp.dot(
            filt[:, h * depth : (h + 1) * depth], rows_in, preferred_element_type=f32
        ).reshape(chans, part, 128)
        out[:, h * part : (h + 1) * part, :] = jnp.where(kept, got, f32(0.0))

    for h in range(2):
        for d in range(1, n_fr):
            share(h, d).wait_send()

    @pl.loop(0, groups)
    def _(g):
        sent = send.at[g, pl.ds(0, n_tm - 1)]
        pltpu.make_async_copy(sent, sent, send_sem.at[g]).wait()


def local(n_tm, n_fr, visibility, codebook, block_index, block_scale, fg_basis, fg_count):
    chans, _, time_dev, base_all = visibility.shape
    modes_all = block_index.shape[0] * n_tm
    bands, codes, block_len, width = codebook.shape
    blocks = base_all // block_len
    all_chans = fg_basis.shape[1]
    groups = base_all // LANES * (chans // SUB)
    wide = blocks * chans
    norm = float(time_dev * n_tm) ** -0.5
    tables = jnp.asarray(phase_tables(n_tm, time_dev, modes_all))
    anywhere = pl.BlockSpec(memory_space=pltpu.HBM)
    f32, bf16 = jnp.float32, jnp.bfloat16
    out = pl.pallas_call(
        functools.partial(kernel, n_tm, n_fr, norm),
        out_shape=jax.ShapeDtypeStruct((chans, bands, width), f32),
        in_specs=[anywhere] * 7,
        out_specs=pl.BlockSpec(memory_space=pltpu.VMEM),
        scratch_shapes=[
            pltpu.VMEM(tables.shape[1:], bf16),
            pltpu.VMEM(codebook.shape, bf16),
            pltpu.VMEM(block_index.shape[1:], jnp.int32),
            pltpu.VMEM(block_scale.shape[1:], f32),
            pltpu.VMEM(fg_basis.shape, f32),
            pltpu.VMEM(tables.shape[1:], f32),
            pltpu.VMEM((1, 1), jnp.int32),
            pltpu.VMEM((DEPTH, BATCH, 2, time_dev, LANES), f32),
            pltpu.VMEM((modes_all, 2 * SUB, LANES), f32),
            pltpu.VMEM((groups, n_tm, 2 * SUB, LANES), bf16),
            pltpu.VMEM((groups, n_tm, 2 * SUB, LANES), bf16),
            pltpu.VMEM((bands, wide), f32),
            pltpu.VMEM((bands, wide), f32),
            pltpu.VMEM((bands, codes // 2 * chans, 2 * wide), bf16),
            pltpu.VMEM((2, blocks, chans, LANES), bf16),
            pltpu.VMEM((bands // 2, codes // 2 * chans, LANES), bf16),
            pltpu.VMEM((chans * (bands // 2), bands * all_chans), bf16),
            pltpu.VMEM((n_fr, bands, chans, width), bf16),
            pltpu.SemaphoreType.DMA((6,)),
            pltpu.SemaphoreType.DMA((DEPTH,)),
            pltpu.SemaphoreType.DMA((groups,)),
            pltpu.SemaphoreType.DMA((groups,)),
            pltpu.SemaphoreType.DMA((2, n_fr - 1)),
            pltpu.SemaphoreType.DMA((2, n_fr - 1)),
        ],
        compiler_params=pltpu.CompilerParams(
            collective_id=0, has_side_effects=True, vmem_limit_bytes=62 * 1024 * 1024
        ),
        name="mmode",
    )(
        tables,
        visibility,
        codebook,
        block_index.reshape(block_index.shape[1:]),
        block_scale.reshape(block_scale.shape[1:]),
        fg_basis,
        fg_count.reshape(1, 1),
    )
    return out[None]


def solution(mesh):
    placed = (
        P("freq", None, "tm", None),
        P(),
        P("tm", "freq", None, None),
        P("tm", "freq", None, None),
        P(),
        P("tm"),
    )
    return jax.shard_map(
        functools.partial(local, mesh.shape["tm"], mesh.shape["freq"]),
        mesh=mesh,
        in_specs=placed,
        out_specs=P("tm", "freq", None, None),
        check_vma=False,
    )
```

```python
import functools
import math

import jax
import jax.numpy as jnp
import numpy as np
from jax import lax
from jax.experimental import pallas as pl
from jax.experimental.pallas import tpu as pltpu
from jax.sharding import PartitionSpec as P

ELLS = 1024
LANES = 512
QUAD = 256
SUB = 8
BATCH = 2
DEPTH = 4
MESH = pl.DeviceIdType.MESH
NT = (((1,), (1,)), ((), ()))


def phase_tables(parts, time_dev, modes_all):
    period = parts * time_dev
    step = 2 * (ELLS // (2 * modes_all)) - 1
    modes = step * np.arange(modes_all, dtype=np.int64)
    times = np.arange(period, dtype=np.int64)
    angle = (modes[:, None] * times[None, :] % period) * (2.0 * math.pi / period)
    cosine = np.cos(angle).reshape(modes_all, parts, time_dev).transpose(1, 0, 2)
    sine = np.sin(angle).reshape(modes_all, parts, time_dev).transpose(1, 0, 2)
    real_rows = np.concatenate([cosine, sine], axis=2)
    imag_rows = np.concatenate([-sine, cosine], axis=2)
    return np.concatenate([real_rows, imag_rows], axis=1).astype(np.float32)


def kernel(
    n_tm, n_fr, norm,
    tab_hbm, vis, cb_hbm, idx_hbm, scl_hbm, bas_hbm, cnt_hbm,
    out,
    tab, cb, idx, scl, bas, tab_in, count, vbuf, acc, send, recv, idx_t, scl_t, sel, vec, comb, filt, gath,
    small_sem, vis_sem, send_sem, recv_sem, gsend_sem, grecv_sem,
):
    tm = lax.axis_index("tm")
    fr = lax.axis_index("freq")
    modes = tab.shape[0] // 2
    samples = vbuf.shape[3]
    chans = vis.shape[0]
    halves = chans // SUB
    lane_groups = vis.shape[3] // LANES
    groups = lane_groups * halves
    piece = min(256, samples)
    blocks = vec.shape[1]
    bands, codes = cb.shape[0], cb.shape[1]
    f32, bf16 = jnp.float32, jnp.bfloat16

    smalls = [
        pltpu.make_async_copy(src, dst, small_sem.at[i])
        for i, (src, dst) in enumerate(
            (
                (idx_hbm, idx), (scl_hbm, scl), (tab_hbm.at[tm], tab_in), (bas_hbm, bas), (cb_hbm, cb),
                (cnt_hbm, count),
            )
        )
    ]

    def fetch(step, slot):
        per_group = SUB // BATCH
        g = step // per_group
        lanes = pl.ds(pl.multiple_of((g // halves) * LANES, LANES), LANES)
        chan = (g % halves) * SUB + (step % per_group) * BATCH
        return pltpu.make_async_copy(
            vis.at[pl.ds(chan, BATCH), :, :, lanes], vbuf.at[slot], vis_sem.at[slot]
        )

    for copy in smalls[:3]:
        copy.start()
    for slot in range(DEPTH):
        fetch(slot, slot).start()
    for copy in smalls[3:]:
        copy.start()

    barrier = pltpu.get_barrier_semaphore()

    @pl.loop(1, n_tm)
    def _(d):
        peer = lax.rem(tm + d, n_tm)
        pl.semaphore_signal(barrier, inc=1, device_id={"tm": peer}, device_id_type=MESH)

    for d in range(1, n_fr):
        peer = lax.rem(fr + d, n_fr)
        pl.semaphore_signal(barrier, inc=1, device_id={"freq": peer}, device_id_type=MESH)

    smalls[0].wait()
    smalls[1].wait()
    wide = blocks * chans
    eye = (
        lax.broadcasted_iota(jnp.int32, (bands, bands), 0)
        == lax.broadcasted_iota(jnp.int32, (bands, bands), 1)
    ).astype(f32).astype(bf16)
    for src, dst in ((idx, idx_t), (scl, scl_t)):
        rows = jnp.concatenate([src[:, j, :] for j in range(blocks)], axis=0)
        rows = rows.astype(f32).astype(bf16)
        dst[...] = lax.dot_general(eye, rows, NT, preferred_element_type=f32)
    same_chan = (
        lax.broadcasted_iota(jnp.int32, (chans, wide), 1) % chans
        == lax.broadcasted_iota(jnp.int32, (chans, wide), 0)
    )

    @pl.loop(0, bands)
    def _(l):
        which = jnp.broadcast_to(idx_t[pl.ds(l, 1), :], (chans, wide))
        which = jnp.where(same_chan, which, f32(-1.0))
        scale = jnp.broadcast_to(scl_t[pl.ds(l, 1), :], (chans, wide))
        for p in range(codes):
            row, col = (p // 2) * chans, (p % 2) * wide
            sel[l, row : row + chans, col : col + wide] = jnp.where(
                which == f32(p), scale, f32(0.0)
            ).astype(bf16)

    smalls[2].wait()
    tab[...] = tab_in[...].astype(bf16)
    pl.semaphore_wait(barrier, n_tm - 1 + n_fr - 1)

    def take(lane_group):
        parts = []
        for half in range(halves):
            g = lane_group * halves + half
            pltpu.make_async_copy(recv.at[g], recv.at[g], recv_sem.at[g]).wait()
            parts.append(jnp.sum(recv[g].astype(f32), axis=0))
        real = jnp.concatenate([part[:SUB] for part in parts], axis=0)
        imag = jnp.concatenate([part[SUB:] for part in parts], axis=0)
        left = lax.broadcasted_iota(jnp.int32, (chans, 128), 1) < 64
        zero = jnp.zeros((chans, 128), f32)
        for pair in range(LANES // 128):
            r = real[:, pair * 128 : pair * 128 + 128]
            i = imag[:, pair * 128 : pair * 128 + 128]
            rr, ri = pltpu.roll(r, 64, 1), pltpu.roll(i, 64, 1)
            even = lane_group * (LANES // 64) + 2 * pair

            def put(first, j, a, b):
                if first:
                    a, b = jnp.where(left, a, zero), jnp.where(left, b, zero)
                else:
                    a, b = jnp.where(left, zero, a), jnp.where(left, zero, b)
                vec[0 if first else 1, j] = jnp.concatenate([a, b], axis=1).astype(bf16)

            put(True, even, r, i)
            put(False, even, rr, ri)
            put(True, even + 1, rr, ri)
            put(False, even + 1, r, i)

    @pl.loop(0, lane_groups)
    def _(lane_group):
        @pl.loop(0, halves)
        def _(half):
            g = lane_group * halves + half
            for part in range(SUB // BATCH):
                step = g * (SUB // BATCH) + part
                slot = lax.rem(step, DEPTH)
                fetch(step, slot).wait()
                for i in range(BATCH):
                    sums = jnp.zeros((2 * modes, LANES), f32)
                    for c in range(2):
                        for t in range(0, samples, piece):
                            block = vbuf[slot, i, c, t : t + piece, :].astype(bf16)
                            table = tab[:, c * samples + t : c * samples + t + piece]
                            sums += jnp.dot(table, block, preferred_element_type=f32)
                    chan = part * BATCH + i
                    acc[:, chan, :] = sums[:modes]
                    acc[:, SUB + chan, :] = sums[modes:]

                @pl.when(step + DEPTH < groups * (SUB // BATCH))
                def _():
                    fetch(step + DEPTH, slot).start()

            send[g] = (acc[...] * f32(norm)).astype(bf16)
            pltpu.make_async_copy(send.at[g, tm], recv.at[g, tm], recv_sem.at[g]).start()

            @pl.loop(1, n_tm)
            def _(d):
                peer = lax.rem(tm + d, n_tm)
                pltpu.make_async_remote_copy(
                    src_ref=send.at[g, peer],
                    dst_ref=recv.at[g, tm],
                    send_sem=send_sem.at[g],
                    recv_sem=recv_sem.at[g],
                    device_id={"tm": peer},
                    device_id_type=MESH,
                ).start()

        @pl.when(lane_group > 0)
        def _():
            take(lane_group - 1)

    smalls[3].wait()
    smalls[4].wait()
    smalls[5].wait()
    part = bands // 2
    all_chans = bas.shape[1]
    rows = chans * part
    pick = (
        lax.broadcasted_iota(jnp.int32, (rows, all_chans), 1)
        == lax.broadcasted_iota(jnp.int32, (rows, all_chans), 0) // part + fr * chans
    ).astype(f32).astype(bf16)
    basis = bas[...].reshape(bands * all_chans, all_chans).astype(bf16)
    spread = lax.dot_general(pick, basis, NT, preferred_element_type=f32)
    same_band = (
        lax.broadcasted_iota(jnp.int32, spread.shape, 1) // all_chans % part
        == lax.broadcasted_iota(jnp.int32, spread.shape, 0) % part
    )
    filt[...] = jnp.where(same_band, spread, f32(0.0)).astype(bf16)

    take(lane_groups - 1)

    vectors = vec[...].reshape(2 * wide, QUAD)
    left = lax.broadcasted_iota(jnp.int32, (chans, 128), 1) < 64
    pairs = codes // 2

    def share(h, d):
        peer = lax.rem(fr + d, n_fr)
        mine = gath.at[fr, pl.ds(h * part, part)]
        return pltpu.make_async_remote_copy(
            src_ref=mine,
            dst_ref=mine,
            send_sem=gsend_sem.at[h, d - 1],
            recv_sem=grecv_sem.at[h, d - 1],
            device_id={"freq": peer},
            device_id_type=MESH,
        )

    for h in range(2):
        chosen = sel[h * part : (h + 1) * part].reshape(part * pairs * chans, 2 * wide)
        comb[...] = (
            jnp.dot(chosen, vectors, preferred_element_type=f32)
            .astype(bf16)
            .reshape(part, pairs * chans, QUAD)
        )
        for k in range(part):
            c = comb[k]
            lhs = jnp.concatenate(
                [
                    jnp.concatenate(
                        [c[p * chans : (p + 1) * chans, o : o + 128] for p in range(pairs)], axis=1
                    )
                    for o in (0, 128)
                ],
                axis=0,
            )
            weights = cb[h * part + k].reshape(codes * 64, 128)
            both = jnp.dot(lhs, weights, preferred_element_type=f32)
            upper, lower = both[:chans], both[chans:]
            projected = jnp.where(left, upper, -upper) + pltpu.roll(lower, 64, 1)
            gath[fr, h * part + k] = projected.astype(bf16)
        for d in range(1, n_fr):
            share(h, d).start()

    mode_index = lax.broadcasted_iota(jnp.int32, (chans, part, 128), 0) + fr * chans
    kept = mode_index >= count[...].reshape(1, 1, 1)
    for h in range(2):
        for d in range(1, n_fr):
            share(h, d).wait_recv()
        rows_in = jnp.concatenate(
            [gath[s, h * part + k] for k in range(part) for s in range(n_fr)], axis=0
        )
        depth = part * all_chans
        got = jnp.dot(
            filt[:, h * depth : (h + 1) * depth], rows_in, preferred_element_type=f32
        ).reshape(chans, part, 128)
        out[:, h * part : (h + 1) * part, :] = jnp.where(kept, got, f32(0.0))

    for h in range(2):
        for d in range(1, n_fr):
            share(h, d).wait_send()

    @pl.loop(0, groups)
    def _(g):
        sent = send.at[g, pl.ds(0, n_tm - 1)]
        pltpu.make_async_copy(sent, sent, send_sem.at[g]).wait()


def local(n_tm, n_fr, visibility, codebook, block_index, block_scale, fg_basis, fg_count):
    chans, _, time_dev, base_all = visibility.shape
    modes_all = block_index.shape[0] * n_tm
    bands, codes, block_len, width = codebook.shape
    blocks = base_all // block_len
    all_chans = fg_basis.shape[1]
    groups = base_all // LANES * (chans // SUB)
    wide = blocks * chans
    norm = float(time_dev * n_tm) ** -0.5
    tables = jnp.asarray(phase_tables(n_tm, time_dev, modes_all))
    anywhere = pl.BlockSpec(memory_space=pltpu.HBM)
    f32, bf16 = jnp.float32, jnp.bfloat16
    out = pl.pallas_call(
        functools.partial(kernel, n_tm, n_fr, norm),
        out_shape=jax.ShapeDtypeStruct((chans, bands, width), f32),
        in_specs=[anywhere] * 7,
        out_specs=pl.BlockSpec(memory_space=pltpu.VMEM),
        scratch_shapes=[
            pltpu.VMEM(tables.shape[1:], bf16),
            pltpu.VMEM(codebook.shape, bf16),
            pltpu.VMEM(block_index.shape[1:], jnp.int32),
            pltpu.VMEM(block_scale.shape[1:], f32),
            pltpu.VMEM(fg_basis.shape, f32),
            pltpu.VMEM(tables.shape[1:], f32),
            pltpu.VMEM((1, 1), jnp.int32),
            pltpu.VMEM((DEPTH, BATCH, 2, time_dev, LANES), f32),
            pltpu.VMEM((modes_all, 2 * SUB, LANES), f32),
            pltpu.VMEM((groups, n_tm, 2 * SUB, LANES), bf16),
            pltpu.VMEM((groups, n_tm, 2 * SUB, LANES), bf16),
            pltpu.VMEM((bands, wide), f32),
            pltpu.VMEM((bands, wide), f32),
            pltpu.VMEM((bands, codes // 2 * chans, 2 * wide), bf16),
            pltpu.VMEM((2, blocks, chans, QUAD), bf16),
            pltpu.VMEM((bands // 2, codes // 2 * chans, QUAD), bf16),
            pltpu.VMEM((chans * (bands // 2), bands * all_chans), bf16),
            pltpu.VMEM((n_fr, bands, chans, width), bf16),
            pltpu.SemaphoreType.DMA((6,)),
            pltpu.SemaphoreType.DMA((DEPTH,)),
            pltpu.SemaphoreType.DMA((groups,)),
            pltpu.SemaphoreType.DMA((groups,)),
            pltpu.SemaphoreType.DMA((2, n_fr - 1)),
            pltpu.SemaphoreType.DMA((2, n_fr - 1)),
        ],
        compiler_params=pltpu.CompilerParams(
            collective_id=0, has_side_effects=True, vmem_limit_bytes=62 * 1024 * 1024
        ),
        name="mmode",
    )(
        tables,
        visibility,
        codebook,
        block_index.reshape(block_index.shape[1:]),
        block_scale.reshape(block_scale.shape[1:]),
        fg_basis,
        fg_count.reshape(1, 1),
    )
    return out[None]


def solution(mesh):
    placed = (
        P("freq", None, "tm", None),
        P(),
        P("tm", "freq", None, None),
        P("tm", "freq", None, None),
        P(),
        P("tm"),
    )
    return jax.shard_map(
        functools.partial(local, mesh.shape["tm"], mesh.shape["freq"]),
        mesh=mesh,
        in_specs=placed,
        out_specs=P("tm", "freq", None, None),
        check_vma=False,
    )
```

```python
import functools
import math

import jax
import jax.numpy as jnp
import numpy as np
from jax import lax
from jax.experimental import pallas as pl
from jax.experimental.pallas import tpu as pltpu
from jax.sharding import PartitionSpec as P

ELLS = 1024
LANES = 256
SUB = 8
BATCH = 4
DEPTH = 4
MESH = pl.DeviceIdType.MESH
NT = (((1,), (1,)), ((), ()))


def phase_tables(parts, time_dev, modes_all):
    period = parts * time_dev
    step = 2 * (ELLS // (2 * modes_all)) - 1
    modes = step * np.arange(modes_all, dtype=np.int64)
    times = np.arange(period, dtype=np.int64)
    angle = (modes[:, None] * times[None, :] % period) * (2.0 * math.pi / period)
    cosine = np.cos(angle).reshape(modes_all, parts, time_dev).transpose(1, 0, 2)
    sine = np.sin(angle).reshape(modes_all, parts, time_dev).transpose(1, 0, 2)
    real_rows = np.concatenate([cosine, sine], axis=2)
    imag_rows = np.concatenate([-sine, cosine], axis=2)
    return np.concatenate([real_rows, imag_rows], axis=1).astype(np.float32)


def kernel(
    n_tm, n_fr, norm,
    tab_hbm, vis, cb_hbm, idx_hbm, scl_hbm, bas_hbm, cnt_hbm,
    out,
    tab, cb, idx, scl, bas, tab_in, count, vbuf, acc, send, recv, idx_t, scl_t, sel, vec, comb, filt, gath,
    small_sem, vis_sem, send_sem, recv_sem, gsend_sem, grecv_sem,
):
    tm = lax.axis_index("tm")
    fr = lax.axis_index("freq")
    modes = tab.shape[0] // 2
    samples = vbuf.shape[3]
    chans = vis.shape[0]
    halves = chans // SUB
    lane_groups = vis.shape[3] // LANES
    groups = lane_groups * halves
    piece = min(256, samples)
    blocks = vec.shape[1]
    bands, codes = cb.shape[0], cb.shape[1]
    f32, bf16 = jnp.float32, jnp.bfloat16

    smalls = [
        pltpu.make_async_copy(src, dst, small_sem.at[i])
        for i, (src, dst) in enumerate(
            (
                (idx_hbm, idx), (scl_hbm, scl), (tab_hbm.at[tm], tab_in), (bas_hbm, bas), (cb_hbm, cb),
                (cnt_hbm, count),
            )
        )
    ]

    def fetch(step, slot):
        per_group = SUB // BATCH
        g = step // per_group
        lanes = pl.ds(pl.multiple_of((g // halves) * LANES, LANES), LANES)
        chan = (g % halves) * SUB + (step % per_group) * BATCH
        return pltpu.make_async_copy(
            vis.at[pl.ds(chan, BATCH), :, :, lanes], vbuf.at[slot], vis_sem.at[slot]
        )

    for copy in smalls[:3]:
        copy.start()
    for slot in range(DEPTH):
        fetch(slot, slot).start()
    for copy in smalls[3:]:
        copy.start()

    barrier = pltpu.get_barrier_semaphore()

    @pl.loop(1, n_tm)
    def _(d):
        peer = lax.rem(tm + d, n_tm)
        pl.semaphore_signal(barrier, inc=1, device_id={"tm": peer}, device_id_type=MESH)

    for d in range(1, n_fr):
        peer = lax.rem(fr + d, n_fr)
        pl.semaphore_signal(barrier, inc=1, device_id={"freq": peer}, device_id_type=MESH)

    smalls[0].wait()
    smalls[1].wait()
    wide = blocks * chans
    eye = (
        lax.broadcasted_iota(jnp.int32, (bands, bands), 0)
        == lax.broadcasted_iota(jnp.int32, (bands, bands), 1)
    ).astype(f32).astype(bf16)
    for src, dst in ((idx, idx_t), (scl, scl_t)):
        rows = jnp.concatenate([src[:, j, :] for j in range(blocks)], axis=0)
        rows = rows.astype(f32).astype(bf16)
        dst[...] = lax.dot_general(eye, rows, NT, preferred_element_type=f32)
    same_chan = (
        lax.broadcasted_iota(jnp.int32, (chans, wide), 1) % chans
        == lax.broadcasted_iota(jnp.int32, (chans, wide), 0)
    )

    @pl.loop(0, bands)
    def _(l):
        which = jnp.broadcast_to(idx_t[pl.ds(l, 1), :], (chans, wide))
        which = jnp.where(same_chan, which, f32(-1.0))
        scale = jnp.broadcast_to(scl_t[pl.ds(l, 1), :], (chans, wide))
        for p in range(codes):
            row, col = (p // 2) * chans, (p % 2) * wide
            sel[l, row : row + chans, col : col + wide] = jnp.where(
                which == f32(p), scale, f32(0.0)
            ).astype(bf16)

    smalls[2].wait()
    tab[...] = tab_in[...].astype(bf16)
    pl.semaphore_wait(barrier, n_tm - 1 + n_fr - 1)

    def take(lane_group):
        parts = []
        for half in range(halves):
            g = lane_group * halves + half
            pltpu.make_async_copy(recv.at[g], recv.at[g], recv_sem.at[g]).wait()
            parts.append(jnp.sum(recv[g].astype(f32), axis=0))
        real = jnp.concatenate([part[:SUB] for part in parts], axis=0)
        imag = jnp.concatenate([part[SUB:] for part in parts], axis=0)
        left = lax.broadcasted_iota(jnp.int32, (chans, 128), 1) < 64
        zero = jnp.zeros((chans, 128), f32)
        for pair in range(LANES // 128):
            r = real[:, pair * 128 : pair * 128 + 128]
            i = imag[:, pair * 128 : pair * 128 + 128]
            rr, ri = pltpu.roll(r, 64, 1), pltpu.roll(i, 64, 1)
            even = lane_group * (LANES // 64) + 2 * pair

            def put(first, j, a, b):
                if first:
                    a, b = jnp.where(left, a, zero), jnp.where(left, b, zero)
                else:
                    a, b = jnp.where(left, zero, a), jnp.where(left, zero, b)
                vec[0 if first else 1, j] = jnp.concatenate([a, b], axis=1).astype(bf16)

            put(True, even, r, i)
            put(False, even, rr, ri)
            put(True, even + 1, rr, ri)
            put(False, even + 1, r, i)

    @pl.loop(0, lane_groups)
    def _(lane_group):
        @pl.loop(0, halves)
        def _(half):
            g = lane_group * halves + half
            for part in range(SUB // BATCH):
                step = g * (SUB // BATCH) + part
                slot = lax.rem(step, DEPTH)
                fetch(step, slot).wait()
                for i in range(BATCH):
                    sums = jnp.zeros((2 * modes, LANES), f32)
                    for c in range(2):
                        for t in range(0, samples, piece):
                            block = vbuf[slot, i, c, t : t + piece, :].astype(bf16)
                            table = tab[:, c * samples + t : c * samples + t + piece]
                            sums += jnp.dot(table, block, preferred_element_type=f32)
                    chan = part * BATCH + i
                    acc[:, chan, :] = sums[:modes]
                    acc[:, SUB + chan, :] = sums[modes:]

                @pl.when(step + DEPTH < groups * (SUB // BATCH))
                def _():
                    fetch(step + DEPTH, slot).start()

            send[g] = (acc[...] * f32(norm)).astype(bf16)
            pltpu.make_async_copy(send.at[g, tm], recv.at[g, tm], recv_sem.at[g]).start()

            @pl.loop(1, n_tm)
            def _(d):
                peer = lax.rem(tm + d, n_tm)
                pltpu.make_async_remote_copy(
                    src_ref=send.at[g, peer],
                    dst_ref=recv.at[g, tm],
                    send_sem=send_sem.at[g],
                    recv_sem=recv_sem.at[g],
                    device_id={"tm": peer},
                    device_id_type=MESH,
                ).start()

        @pl.when(lane_group > 0)
        def _():
            take(lane_group - 1)

    smalls[3].wait()
    smalls[4].wait()
    smalls[5].wait()
    part = bands // 2
    all_chans = bas.shape[1]
    rows = chans * part
    pick = (
        lax.broadcasted_iota(jnp.int32, (rows, all_chans), 1)
        == lax.broadcasted_iota(jnp.int32, (rows, all_chans), 0) // part + fr * chans
    ).astype(f32).astype(bf16)
    basis = bas[...].reshape(bands * all_chans, all_chans).astype(bf16)
    spread = lax.dot_general(pick, basis, NT, preferred_element_type=f32)
    same_band = (
        lax.broadcasted_iota(jnp.int32, spread.shape, 1) // all_chans % part
        == lax.broadcasted_iota(jnp.int32, spread.shape, 0) % part
    )
    filt[...] = jnp.where(same_band, spread, f32(0.0)).astype(bf16)

    take(lane_groups - 1)

    vectors = vec[...].reshape(2 * wide, LANES)
    left = lax.broadcasted_iota(jnp.int32, (chans, 128), 1) < 64
    pairs = codes // 2

    def share(h, d):
        peer = lax.rem(fr + d, n_fr)
        mine = gath.at[fr, pl.ds(h * part, part)]
        return pltpu.make_async_remote_copy(
            src_ref=mine,
            dst_ref=mine,
            send_sem=gsend_sem.at[h, d - 1],
            recv_sem=grecv_sem.at[h, d - 1],
            device_id={"freq": peer},
            device_id_type=MESH,
        )

    for h in range(2):
        chosen = sel[h * part : (h + 1) * part].reshape(part * pairs * chans, 2 * wide)
        comb[...] = (
            jnp.dot(chosen, vectors, preferred_element_type=f32)
            .astype(bf16)
            .reshape(part, pairs * chans, LANES)
        )
        for k in range(part):
            c = comb[k]
            lhs = jnp.concatenate(
                [
                    jnp.concatenate(
                        [c[p * chans : (p + 1) * chans, o : o + 128] for p in range(pairs)], axis=1
                    )
                    for o in (0, 128)
                ],
                axis=0,
            )
            weights = cb[h * part + k].reshape(codes * 64, 128)
            both = jnp.dot(lhs, weights, preferred_element_type=f32)
            upper, lower = both[:chans], both[chans:]
            projected = jnp.where(left, upper, -upper) + pltpu.roll(lower, 64, 1)
            gath[fr, h * part + k] = projected.astype(bf16)
        for d in range(1, n_fr):
            share(h, d).start()

    mode_index = lax.broadcasted_iota(jnp.int32, (chans, part, 128), 0) + fr * chans
    kept = mode_index >= count[...].reshape(1, 1, 1)
    for h in range(2):
        for d in range(1, n_fr):
            share(h, d).wait_recv()
        rows_in = jnp.concatenate(
            [gath[s, h * part + k] for k in range(part) for s in range(n_fr)], axis=0
        )
        depth = part * all_chans
        got = jnp.dot(
            filt[:, h * depth : (h + 1) * depth], rows_in, preferred_element_type=f32
        ).reshape(chans, part, 128)
        out[:, h * part : (h + 1) * part, :] = jnp.where(kept, got, f32(0.0))

    for h in range(2):
        for d in range(1, n_fr):
            share(h, d).wait_send()

    @pl.loop(0, groups)
    def _(g):
        sent = send.at[g, pl.ds(0, n_tm - 1)]
        pltpu.make_async_copy(sent, sent, send_sem.at[g]).wait()


def local(n_tm, n_fr, visibility, codebook, block_index, block_scale, fg_basis, fg_count):
    chans, _, time_dev, base_all = visibility.shape
    modes_all = block_index.shape[0] * n_tm
    bands, codes, block_len, width = codebook.shape
    blocks = base_all // block_len
    all_chans = fg_basis.shape[1]
    groups = base_all // LANES * (chans // SUB)
    wide = blocks * chans
    norm = float(time_dev * n_tm) ** -0.5
    tables = jnp.asarray(phase_tables(n_tm, time_dev, modes_all))
    anywhere = pl.BlockSpec(memory_space=pltpu.HBM)
    f32, bf16 = jnp.float32, jnp.bfloat16
    out = pl.pallas_call(
        functools.partial(kernel, n_tm, n_fr, norm),
        out_shape=jax.ShapeDtypeStruct((chans, bands, width), f32),
        in_specs=[anywhere] * 7,
        out_specs=pl.BlockSpec(memory_space=pltpu.VMEM),
        scratch_shapes=[
            pltpu.VMEM(tables.shape[1:], bf16),
            pltpu.VMEM(codebook.shape, bf16),
            pltpu.VMEM(block_index.shape[1:], jnp.int32),
            pltpu.VMEM(block_scale.shape[1:], f32),
            pltpu.VMEM(fg_basis.shape, f32),
            pltpu.VMEM(tables.shape[1:], f32),
            pltpu.VMEM((1, 1), jnp.int32),
            pltpu.VMEM((DEPTH, BATCH, 2, time_dev, LANES), f32),
            pltpu.VMEM((modes_all, 2 * SUB, LANES), f32),
            pltpu.VMEM((groups, n_tm, 2 * SUB, LANES), bf16),
            pltpu.VMEM((groups, n_tm, 2 * SUB, LANES), bf16),
            pltpu.VMEM((bands, wide), f32),
            pltpu.VMEM((bands, wide), f32),
            pltpu.VMEM((bands, codes // 2 * chans, 2 * wide), bf16),
            pltpu.VMEM((2, blocks, chans, LANES), bf16),
            pltpu.VMEM((bands // 2, codes // 2 * chans, LANES), bf16),
            pltpu.VMEM((chans * (bands // 2), bands * all_chans), bf16),
            pltpu.VMEM((n_fr, bands, chans, width), bf16),
            pltpu.SemaphoreType.DMA((6,)),
            pltpu.SemaphoreType.DMA((DEPTH,)),
            pltpu.SemaphoreType.DMA((groups,)),
            pltpu.SemaphoreType.DMA((groups,)),
            pltpu.SemaphoreType.DMA((2, n_fr - 1)),
            pltpu.SemaphoreType.DMA((2, n_fr - 1)),
        ],
        compiler_params=pltpu.CompilerParams(
            collective_id=0, has_side_effects=True, vmem_limit_bytes=55040 * 1024
        ),
        name="mmode",
    )(
        tables,
        visibility,
        codebook,
        block_index.reshape(block_index.shape[1:]),
        block_scale.reshape(block_scale.shape[1:]),
        fg_basis,
        fg_count.reshape(1, 1),
    )
    return out[None]


def solution(mesh):
    placed = (
        P("freq", None, "tm", None),
        P(),
        P("tm", "freq", None, None),
        P("tm", "freq", None, None),
        P(),
        P("tm"),
    )
    return jax.shard_map(
        functools.partial(local, mesh.shape["tm"], mesh.shape["freq"]),
        mesh=mesh,
        in_specs=placed,
        out_specs=P("tm", "freq", None, None),
        check_vma=False,
    )
```
